512 devices in a mesh: row: 32 (over x, z_lo), col: 16 (over y, z_hi, core).
Axes of the slice: x: 4, y: 4, z: 16 (z_hi: 2, z_lo: 8; z = z_hi * 8 + z_lo), core: 2. Of those that a mesh axis runs over, the one named last changes fastest.
Arguments:
- density: bfloat16 [256, 16, 2, 128, 128], P('row', 'col'), may hold values from -0.26953125 to 0.26953125
- pattern: int32 [256, 16, 2], P('row', 'col'), may hold values from 0 to 15, as said below
- kept_pattern: int32 [256, 16, 4], P('row', 'col'), may hold values from 0 to 15, as said below
Outputs:
- purified: bfloat16 [256, 16, 4, 128, 128], P('row', 'col')
The draws below stay inside these ranges and needn't reach their ends.
Inputs may be any that keep to these rules, and one draw needn't show every extreme that they name: `pattern`: in each block row and tile the 2 entries are distinct block columns of that tile, numbered within it. `kept_pattern`: in each block row and tile the 4 entries are distinct block columns of that tile, numbered within it.
All inputs are finite; a program needn't handle non-finite values.
Results may differ from the reference program's by a relative error of at most 0.005.
Values may be sent and summed in bfloat16 or wider, within the bound.
A program may use at most 64 MiB of HBM per device.

```python
import jax
import jax.numpy as jnp
from jax import lax

BS = 128
BR = 8
KS = 2
KF = 4
ST = 4
NB = 256
TILE_COLS = 16
TILE_W = 16
N_ROW = 32
N_COL = 16


def distinct_picks(key, count):
    scores = jax.random.randint(key, (NB, TILE_COLS, TILE_W), 0, 1 << 20) * TILE_W + jnp.arange(TILE_W, dtype=jnp.int32)
    return lax.top_k(scores, count)[1].astype(jnp.int32)


def draw_pattern(key, part):
    key = jax.random.fold_in(key, 11)
    return distinct_picks(key, KS)


def draw_kept_pattern(key, part):
    key = jax.random.fold_in(key, 23)
    return distinct_picks(key, KF)


def shard_levels(own_key, shape, shards, smallest, top_value):
    def one(position, shards_of):
        heights = jax.random.uniform(jax.random.fold_in(jax.random.fold_in(own_key, 6), position), (shards_of,), jnp.float32, smallest / len(shards), top_value / len(shards))
        return jnp.repeat(jnp.exp(heights), shape[position] // shards_of).reshape((-1,) + (1,) * (len(shape) - position - 1))

    level = one(*shards[0])
    for cut in shards[1:]:
        level = level * one(*cut)
    return level


def noise(key, shape, spread, most, cuts=(), kind=jnp.bfloat16):
    gain = shard_levels(key, shape, cuts, -0.22, 0.18) if cuts else 1.0
    entries = jax.random.normal(key, shape, jnp.float32) * spread * gain
    return jnp.minimum(jnp.maximum(entries, -most), most).astype(kind)


def setup_inputs(seed: int = 0) -> dict:
    key_of = jax.random.split(jax.random.key(seed), 4)
    return {
        "density": noise(key_of[0], (NB, TILE_COLS, KS, BS, BS), 0.045, 0.26953125, ((0, 32), (1, 16))),
        "pattern": draw_pattern(jax.random.fold_in(key_of[3], 71), 0),
        "kept_pattern": draw_kept_pattern(jax.random.fold_in(key_of[3], 71), 0),
    }


def windowed_product(left_blocks, left_index, right_blocks, right_index, kept_index):
    tile_width = (N_ROW // N_COL) * BR
    columns = jnp.arange(N_COL, dtype=jnp.int32)

    def one_row(block_row):
        row_blocks = left_blocks[block_row]
        row_index = left_index[block_row]
        row_kept = kept_index[block_row]
        summed = jnp.zeros((N_COL, row_kept.shape[1], BS, BS), jnp.float32)
        for section_num in range(ST):
            group = (columns + section_num) % N_COL
            blocks = row_blocks[group]
            index = row_index[group]
            inner = group[:, None] * tile_width + index
            picked = right_blocks[inner, columns[:, None]]
            picked_index = right_index[inner, columns[:, None]]
            products = jnp.einsum("cixy,cijyz->cijxz", blocks.astype(jnp.float32), picked.astype(jnp.float32), precision=lax.Precision.HIGHEST)
            matches = (picked_index[..., None] == row_kept[:, None, None, :]).astype(jnp.float32)
            summed = summed + jnp.einsum("cijt,cijxz->ctxz", matches, products, precision=lax.Precision.HIGHEST)
        return summed

    return lax.map(one_row, jnp.arange(NB, dtype=jnp.int32))


def reference(density, pattern, kept_pattern):
    squared = windowed_product(density, pattern, density, pattern, kept_pattern).astype(jnp.bfloat16)
    cubed = windowed_product(squared, kept_pattern, density, pattern, kept_pattern)
    return (3.0 * squared.astype(jnp.float32) - 2.0 * cubed).astype(jnp.bfloat16)
```

```python
import functools

import jax
import jax.numpy as jnp
from jax import lax
from jax.experimental import pallas as pl
from jax.experimental.pallas import tpu as pltpu
from jax.sharding import PartitionSpec as P

MESH = pl.DeviceIdType.MESH
ROWS, COLS = 32, 16
NX, NZ = 4, 8
BS = 128
META = 48
ZERO = 128


def place():
    r, c = lax.axis_index("row"), lax.axis_index("col")
    return r, c, r // NZ, r % NZ, c % 2


def remote(src, dst, send, recv, device):
    return pltpu.make_async_remote_copy(
        src_ref=src, dst_ref=dst, send_sem=send, recv_sem=recv, device_id=device, device_id_type=MESH
    )


def gather_kernel(
    d, left, right, s_scat, r_scat, s_z, r_z, s_x, r_x, s_h, r_h, s_cross, r_cross, s_left, r_left, local
):
    r, c, x, z, kap = place()
    sib = c + 1 - 2 * kap
    xr, xl, xo = (x + 1) % NX, (x + 3) % NX, (x + 2) % NX
    up, down = z < NZ - 1, z > 0
    source = ((r - 2 * c + ROWS) % ROWS < 8, (r - 2 * c - 4 + 2 * ROWS) % ROWS < 8)
    back2, back3, back4 = (c + 14) % COLS, (c + 13) % COLS, (c + 12) % COLS
    third = (c + jnp.where(kap == 0, 13, 3)) % COLS

    barrier = pltpu.get_barrier_semaphore()

    def greet(device):
        pl.semaphore_signal(barrier, inc=1, device_id=device, device_id_type=MESH)

    for column in (back2, (c + 2) % COLS, back4, (c + 4) % COLS, sib, third):
        greet((r, column))
    for other in (xr, xl, xo):
        greet((other * NZ + z, c))

    @pl.when(up)
    def _():
        greet((r + 1, c))

    @pl.when(down)
    def _():
        greet((r - 1, c))

    pl.semaphore_wait(barrier, 9 + up.astype(jnp.int32) + down.astype(jnp.int32))

    def cross(u):
        part = pl.ds(4 * u, 4)
        return remote(d.at[part], left.at[1, part], s_cross.at[u], r_cross.at[u], (r, back2))

    def scatter(tile, step):
        other = (x + step) % NX
        part = pl.ds(4 * other, 4)
        src = d if tile == 0 else left.at[1]
        return remote(
            src.at[part], right.at[tile, z, part], s_scat.at[tile, step - 1], r_scat.at[tile], (other * NZ + z, c)
        )

    def keep(tile):
        part = pl.ds(4 * x, 4)
        src = d if tile == 0 else left.at[1]
        return pltpu.make_async_copy(src.at[part], right.at[tile, z, part], local.at[tile])

    def along_z(tile, piece, way):
        part = right.at[tile, piece, pl.ds(4 * x, 4)]
        to = r + 1 if way == 0 else r - 1
        return remote(part, part, s_z.at[tile, piece, way], r_z.at[tile, piece], (to, c))

    def along_x(tile, piece, way):
        part = right.at[tile, piece, pl.ds(4 * x, 4)]
        to = xr if way == 0 else xl
        return remote(part, part, s_x.at[tile, piece, way], r_x.at[tile, piece, way], (to * NZ + z, c))

    def came_x(tile, piece, way):
        part = right.at[tile, piece, pl.ds(4 * (xl if way == 0 else xr), 4)]
        return remote(part, part, s_x.at[tile, piece, way], r_x.at[tile, piece, way], (r, c))

    def half_x(tile, piece, way):
        part = right.at[tile, piece, pl.ds(4 * xl if way == 0 else 4 * xr + 2, 2)]
        to = xr if way == 0 else xl
        return remote(part, part, s_h.at[tile, piece, way], r_h.at[tile, piece, way], (to * NZ + z, c))

    def came_half(tile, piece, way):
        part = right.at[tile, piece, pl.ds(4 * xo + 2 * way, 2)]
        return remote(part, part, s_h.at[tile, piece, way], r_h.at[tile, piece, way], (r, c))

    def begin(tile):
        @pl.when(source[tile])
        def _():
            keep(tile).wait()

        @pl.when(jnp.logical_not(source[tile]))
        def _():
            part = right.at[tile, z, pl.ds(4 * x, 4)]
            remote(part, part, s_scat.at[tile, 0], r_scat.at[tile], (r, c)).wait_recv()

        @pl.when(up)
        def _():
            along_z(tile, z, 0).start()

        @pl.when(down)
        def _():
            along_z(tile, z, 1).start()

        along_x(tile, z, 0).start()
        along_x(tile, z, 1).start()

    def z_step(tile, step):
        for way in (0, 1):
            piece = z - step if way == 0 else z + step
            onward = up if way == 0 else down

            @pl.when(piece >= 0 if way == 0 else piece < NZ)
            def _():
                along_z(tile, piece, way).wait_recv()

                @pl.when(onward)
                def _():
                    along_z(tile, piece, way).start()

                along_x(tile, piece, 0).start()
                along_x(tile, piece, 1).start()

    def x_step(tile, piece):
        for way in (0, 1):
            came_x(tile, piece, way).wait_recv()
            half_x(tile, piece, way).start()

    def x_round(tile, step):
        for way in (0, 1):
            piece = z - step if way == 0 else z + step

            @pl.when(piece >= 0 if way == 0 else piece < NZ)
            def _():
                x_step(tile, piece)

    def begin_cross():
        for u in range(4):
            cross(u).start()

    def end_cross():
        for u in range(4):
            cross(u).wait_recv()

    def send_y():
        return remote(d, left.at[3], s_left.at[0], r_left.at[3], (r, back4))

    def send_own():
        return remote(d, left.at[0], s_left.at[1], r_left.at[0], (r, sib))

    def pass_cross():
        return remote(left.at[1], left.at[2 * kap], s_left.at[2], r_left.at[2 * kap], (r, sib))

    def pass_cross_y():
        return remote(left.at[1], left.at[4], s_left.at[3], r_left.at[4], (r, back3))

    def pass_y():
        return remote(left.at[3], left.at[2 + 2 * kap], s_left.at[4], r_left.at[2 + 2 * kap], (r, sib))

    @pl.when(source[0])
    def _():
        keep(0).start()
        begin_cross()
        for step in (1, 2, 3):
            scatter(0, step).start()

    send_y().start()

    @pl.when(kap == 1)
    def _():
        send_own().start()

    begin(0)
    z_step(0, 1)

    @pl.when(jnp.logical_not(source[0]))
    def _():
        begin_cross()

    z_step(0, 2)
    z_step(0, 3)

    @pl.when(source[1])
    def _():
        end_cross()
        keep(1).start()
        for step in (1, 2, 3):
            scatter(1, step).start()

    @pl.loop(4, NZ)
    def _(step):
        z_step(0, step)

    send_y().wait_recv()
    pass_y().start()
    begin(1)
    x_step(0, z)

    @pl.loop(1, NZ)
    def _(step):
        z_step(1, step)
        x_round(0, step)

    @pl.when(jnp.logical_not(source[1]))
    def _():
        end_cross()

    pass_cross().start()

    @pl.when(kap == 0)
    def _():
        pass_cross_y().start()

    x_step(1, z)

    @pl.loop(1, NZ)
    def _(step):
        x_round(1, step)

    @pl.loop(0, NZ)
    def _(piece):
        for tile in (0, 1):
            for way in (0, 1):
                came_half(tile, piece, way).wait_recv()
                along_x(tile, piece, way).wait_send()
                half_x(tile, piece, way).wait_send()

            @pl.when(jnp.logical_and(up, piece <= z))
            def _():
                along_z(tile, piece, 0).wait_send()

            @pl.when(jnp.logical_and(down, piece >= z))
            def _():
                along_z(tile, piece, 1).wait_send()

    for slot in (0, 2, 4):
        remote(left.at[slot], left.at[slot], s_left.at[0], r_left.at[slot], (r, c)).wait_recv()
    for u in range(4):
        cross(u).wait_send()
    for tile in (0, 1):

        @pl.when(source[tile])
        def _():
            for step in (1, 2, 3):
                scatter(tile, step).wait_send()

    send_y().wait_send()
    pass_cross().wait_send()
    pass_y().wait_send()

    @pl.when(kap == 1)
    def _():
        send_own().wait_send()

    @pl.when(kap == 0)
    def _():
        pass_cross_y().wait_send()


def product_kernel(meta, d, left, right, out, lv, rv0, rv1, sv, acc, loads, s_sq, r_sq):
    r, c, x, z, kap = place()
    sib = c + 1 - 2 * kap
    back3 = (c + 13) % COLS
    third = (c + jnp.where(kap == 0, 13, 3)) % COLS
    barrier = pltpu.get_barrier_semaphore()
    for column in (sib, third):
        pl.semaphore_signal(barrier, inc=1, device_id=(r, column), device_id_type=MESH)

    copies = [
        pltpu.make_async_copy(d, lv.at[0], loads.at[0]),
        pltpu.make_async_copy(left, lv.at[pl.ds(1, 5)], loads.at[1]),
        pltpu.make_async_copy(right.at[pl.ds(0, 128)], rv0.at[pl.ds(0, 128)], loads.at[2]),
        pltpu.make_async_copy(right.at[pl.ds(128, 128)], rv1.at[pl.ds(0, 128)], loads.at[3]),
    ]
    for copy in copies:
        copy.start()
    for rv in (rv0, rv1):
        rv[ZERO] = jnp.zeros((BS, BS), jnp.bfloat16)
    pl.semaphore_wait(barrier, 2)

    def picks(tile, section, inner, kept):
        column = (c + 2 * tile) % COLS
        group = (2 * column + 2 * section + (inner >> 3)) % ROWS
        row = 2 * (inner & 7)
        at = (group * COLS + column) * META + row
        first, second = meta[at], meta[at + 1]
        base = (group % NZ) * 16 + row
        return [
            jnp.where(first == wanted, base, jnp.where(second == wanted, base + 1, ZERO)) for wanted in kept
        ]

    def kept_of(column, a):
        at = (r * COLS + column) * META + 16 + 4 * a
        return [meta[at + t] for t in range(4)]

    def terms(total, lefts, rv, spots):
        lhs = jnp.concatenate(lefts, axis=1)
        parts = []
        for pair in (0, 2):
            rhs = jnp.concatenate(
                [jnp.concatenate([rv[spot[pair]], rv[spot[pair + 1]]], axis=1) for spot in spots], axis=0
            )
            parts.append(jnp.dot(lhs, rhs, preferred_element_type=jnp.float32))
        return parts if total is None else [old + new for old, new in zip(total, parts)]

    def send(tile, a):
        slot = jnp.where(kap == 0, 3 - 2 * tile, 1 + 2 * tile)
        to = sib if tile == 1 else jnp.where(kap == 0, back3, sib)
        rows = pl.ds(4 * a, 4)
        return remote(
            sv.at[2 * tile, rows], sv.at[slot, rows], s_sq.at[tile, a], r_sq.at[slot, a], (r, to)
        )

    def came(slot, a):
        rows = pl.ds(4 * a, 4)
        return remote(sv.at[slot, rows], sv.at[slot, rows], s_sq.at[0, a], r_sq.at[slot, a], (r, c))

    def square(tile, a):
        kept = kept_of((c + 2 * tile) % COLS, a)
        total = None
        for section in range(4):
            owner = (r * COLS + (c + 2 * tile + section) % COLS) * META + 2 * a
            spots = [picks(tile, section, meta[owner + i], kept) for i in range(2)]
            total = terms(total, [lv[2 * tile + section, 2 * a + i] for i in range(2)], rv1 if tile else rv0, spots)
        for t in range(4):
            sv[2 * tile, 4 * a + t] = total[t // 2][:, (t % 2) * BS : (t % 2 + 1) * BS].astype(jnp.bfloat16)
        send(tile, a).start()

    def cube(sections, a, total):
        kept = kept_of(c, a)
        for section in sections:
            inner = kept_of((c + section) % COLS, a)
            for i in (0, 2):
                spots = [picks(0, section, inner[i + e], kept) for e in range(2)]
                total = terms(total, [sv[section, 4 * a + i + e] for e in range(2)], rv0, spots)
        return total

    copies[0].wait()
    copies[1].wait()
    copies[2].wait()

    @pl.loop(0, 8)
    def _(a):
        square(0, a)

    copies[3].wait()

    @pl.loop(0, 8)
    def _(a):
        square(1, a)

    @pl.loop(0, 8)
    def _(a):
        total = cube((0, 2), a, None)
        acc[a, 0] = total[0]
        acc[a, 1] = total[1]

    @pl.loop(0, 8)
    def _(a):
        came(1, a).wait_recv()
        came(3, a).wait_recv()
        total = cube((1, 3), a, [acc[a, 0], acc[a, 1]])
        for t in range(4):
            part = total[t // 2][:, (t % 2) * BS : (t % 2 + 1) * BS]
            out[4 * a + t] = (3.0 * sv[0, 4 * a + t].astype(jnp.float32) - 2.0 * part).astype(jnp.bfloat16)

    @pl.loop(0, 8)
    def _(a):
        send(0, a).wait_send()
        send(1, a).wait_send()


def on_device(density, pattern, kept_pattern):
    own = density.reshape(16, BS, BS)
    meta = jnp.concatenate([pattern.reshape(16), kept_pattern.reshape(32)])
    meta = lax.all_gather(meta, ("row", "col"), tiled=True)
    dma = pltpu.SemaphoreType.DMA
    left, right = pl.pallas_call(
        gather_kernel,
        out_shape=(
            jax.ShapeDtypeStruct((5, 16, BS, BS), jnp.bfloat16),
            jax.ShapeDtypeStruct((2, NZ, 16, BS, BS), jnp.bfloat16),
        ),
        in_specs=[pl.BlockSpec(memory_space=pl.ANY)],
        out_specs=(pl.BlockSpec(memory_space=pl.ANY),) * 2,
        scratch_shapes=[
            dma((2, 3)),
            dma((2,)),
            dma((2, NZ, 2)),
            dma((2, NZ)),
            dma((2, NZ, 2)),
            dma((2, NZ, 2)),
            dma((2, NZ, 2)),
            dma((2, NZ, 2)),
            dma((4,)),
            dma((4,)),
            dma((5,)),
            dma((5,)),
            dma((2,)),
        ],
        compiler_params=pltpu.CompilerParams(collective_id=0, has_side_effects=True),
        cost_estimate=pl.CostEstimate(flops=0, bytes_accessed=300 << 20, transcendentals=0),
        name="gather_blocks",
    )(own)
    out = pl.pallas_call(
        product_kernel,
        out_shape=jax.ShapeDtypeStruct((32, BS, BS), jnp.bfloat16),
        in_specs=[pl.BlockSpec(memory_space=pltpu.SMEM)] + [pl.BlockSpec(memory_space=pl.ANY)] * 3,
        out_specs=pl.BlockSpec(memory_space=pltpu.VMEM),
        scratch_shapes=[
            pltpu.VMEM((6, 16, BS, BS), jnp.bfloat16),
            pltpu.VMEM((ZERO + 1, BS, BS), jnp.bfloat16),
            pltpu.VMEM((ZERO + 1, BS, BS), jnp.bfloat16),
            pltpu.VMEM((4, 32, BS, BS), jnp.bfloat16),
            pltpu.VMEM((8, 2, BS, 2 * BS), jnp.float32),
            dma((4,)),
            dma((2, 8)),
            dma((4, 8)),
        ],
        compiler_params=pltpu.CompilerParams(
            collective_id=1, has_side_effects=True, vmem_limit_bytes=40 << 20
        ),
        cost_estimate=pl.CostEstimate(flops=4 << 30, bytes_accessed=12 << 20, transcendentals=0),
        name="square_and_cube",
    )(meta, own, left, right.reshape(256, BS, BS))
    return out.reshape(8, 1, 4, BS, BS)


def solution(mesh):
    in_specs = (P("row", "col", None, None, None), P("row", "col", None), P("row", "col", None))
    out_specs = P("row", "col", None, None, None)
    return jax.shard_map(
        on_device, mesh=mesh, in_specs=in_specs, out_specs=out_specs, check_vma=False
    )
```

```python
import jax
import jax.numpy as jnp
from jax import lax
from jax.experimental import pallas as pl
from jax.experimental.pallas import tpu as pltpu
from jax.sharding import PartitionSpec as P

MESH = pl.DeviceIdType.MESH
ROWS, COLS = 32, 16
NX, NZ = 4, 8
BS = 128
ZERO = 128
LAG = 2
CROSS_AT = (0, 0, 0, 0)
PARTS = 3


def remote(src, dst, send, recv, device):
    return pltpu.make_async_remote_copy(
        src_ref=src, dst_ref=dst, send_sem=send, recv_sem=recv, device_id=device, device_id_type=MESH
    )


def kernel(
    meta, d, out,
    left, rv0, rv1, sv, acc, ml, m0, m1, tl, t0, t1,
    s_sc, s_scm, r_sc, local,
    s_z, r_z, s_zm, r_zm,
    s_a, r_a, s_b, r_b, s_am, r_am,
    s_x0, r_x0, s_h0, r_h0, s_x1, r_x1, s_h1, r_h1,
    s_cr, r_cr, s_l, r_l, s_ml, r_ml, s_sq, r_sq,
):
    r, c = lax.axis_index("row"), lax.axis_index("col")
    x, z, kap = r // NZ, r % NZ, c % 2
    sib = c + 1 - 2 * kap
    xr, xl, xo = (x + 1) % NX, (x + 3) % NX, (x + 2) % NX
    up, down = z < NZ - 1, z > 0
    source = (r - 2 * c + ROWS) % ROWS < NZ
    edge = x * NZ + NZ - 1 - z

    def back(steps):
        return (c + COLS - steps) % COLS

    barrier = pltpu.get_barrier_semaphore()

    def greet(device):
        pl.semaphore_signal(barrier, inc=1, device_id=device, device_id_type=MESH)

    for steps in range(1, 6):
        greet((r, back(steps)))
        greet((r, (c + steps) % COLS))
    for other in (xr, xl, xo):
        greet((other * NZ + z, c))

    @pl.when(up)
    def _():
        greet((r + 1, c))

    @pl.when(down)
    def _():
        greet((r - 1, c))

    @pl.when(jnp.logical_not(jnp.logical_and(up, down)))
    def _():
        greet((edge, back(2)))
        greet((edge, (c + 2) % COLS))

    inside = jnp.logical_and(up, down)
    pl.semaphore_wait(barrier, jnp.where(inside, 15, 16))


    def quarter(buffer, piece, which, start=0, size=4):
        return buffer.at[pl.ds(piece * 16 + 4 * which + start, size)]

    def scatter(step):
        other = (x + step) % NX
        to = (other * NZ + z, c)
        return (
            remote(d.at[pl.ds(4 * other, 4)], quarter(rv0, z, other), s_sc.at[step - 1], r_sc.at[0], to),
            remote(meta, m0.at[z], s_scm.at[step - 1], r_sc.at[1], to),
        )

    def keep():
        return (
            pltpu.make_async_copy(d.at[pl.ds(4 * x, 4)], quarter(rv0, z, x), local.at[0]),
            pltpu.make_async_copy(meta, m0.at[z], local.at[1]),
        )

    def along_z(piece, way):
        part = quarter(rv0, piece, x)
        to = (r + 1 if way == 0 else r - 1, c)
        return (
            remote(part, part, s_z.at[piece, way], r_z.at[piece], to),
            remote(m0.at[piece], m0.at[piece], s_zm.at[piece, way], r_zm.at[piece], to),
        )

    def chain(piece, way):
        part = quarter(rv1, piece, x, 2 * way, 2)
        send, recv = (s_a, r_a) if way == 0 else (s_b, r_b)
        copies = [remote(part, part, send.at[piece], recv.at[piece], (r + 1 if way == 0 else r - 1, c))]
        if way == 0:
            copies.append(remote(m1.at[piece], m1.at[piece], s_am.at[piece], r_am.at[piece], (r + 1, c)))
        return copies

    def inject(piece, way):
        send, recv = (s_a, r_a) if way == 0 else (s_b, r_b)
        to = (edge, back(2))
        copies = [
            remote(
                quarter(rv0, piece, x, 2 * way, 2),
                quarter(rv1, piece, x, 2 * way, 2),
                send.at[piece],
                recv.at[piece],
                to,
            )
        ]
        if way == 0:
            copies.append(remote(m0.at[piece], m1.at[piece], s_am.at[piece], r_am.at[piece], to))
        return copies

    def ring(way):
        return ((xr if way == 0 else xl) * NZ + z, c)

    def along_x0(piece, way):
        part = quarter(rv0, piece, x)
        return remote(part, part, s_x0.at[piece, way], r_x0.at[piece, way], ring(way))

    def came_x0(piece, way):
        part = quarter(rv0, piece, xl if way == 0 else xr)
        return remote(part, part, s_x0.at[piece, way], r_x0.at[piece, way], ring(way))

    def along_x1(piece, half, way):
        part = quarter(rv1, piece, x, 2 * half, 2)
        return remote(part, part, s_x1.at[piece, half, way], r_x1.at[piece, half, way], ring(way))

    def came_x1(piece, half, way):
        part = quarter(rv1, piece, xl if way == 0 else xr, 2 * half, 2)
        return remote(part, part, s_x1.at[piece, half, way], r_x1.at[piece, half, way], ring(way))

    def onward(buffer, send, recv, piece, way):
        part = quarter(buffer, piece, xl if way == 0 else xr, 2 * way, 2)
        return remote(part, part, send.at[piece, way], recv.at[piece, way], ring(way))

    def came_onward(buffer, send, recv, piece, way):
        part = quarter(buffer, piece, xo, 2 * way, 2)
        return remote(part, part, send.at[piece, way], recv.at[piece, way], ring(way))

    def cross(u):
        part = pl.ds(4 * u, 4)
        return remote(d.at[part], left.at[1, part], s_cr.at[u], r_cr.at[u], (r, back(2)))

    def send_y():
        return remote(d, left.at[3], s_l.at[0], r_l.at[3], (r, back(4)))

    def send_own():
        return remote(d, left.at[0], s_l.at[1], r_l.at[0], (r, sib))

    def pass_cross():
        return remote(left.at[1], left.at[2 * kap], s_l.at[2], r_l.at[2 * kap], (r, sib))

    def pass_cross_y():
        return remote(left.at[1], left.at[4], s_l.at[3], r_l.at[4], (r, back(3)))

    def pass_y():
        return remote(left.at[3], left.at[2 + 2 * kap], s_l.at[4], r_l.at[2 + 2 * kap], (r, sib))

    def came_left(slot):
        return remote(left.at[slot], left.at[slot], s_l.at[0], r_l.at[slot], (r, sib))

    def send_meta(steps):
        return remote(meta, ml.at[steps], s_ml.at[steps - 1], r_ml.at[steps - 1], (r, back(steps)))


    def arrived0(piece):
        along_x0(piece, 0).start()
        along_x0(piece, 1).start()

        @pl.when(jnp.logical_not(up))
        def _():
            for copy in inject(piece, 0):
                copy.start()

        @pl.when(jnp.logical_not(down))
        def _():
            for copy in inject(piece, 1):
                copy.start()

    def z_step(k):
        for way in (0, 1):
            piece = z - k if way == 0 else z + k

            @pl.when(piece >= 0 if way == 0 else piece < NZ)
            def _():
                copies = along_z(piece, way)
                for copy in copies:
                    copy.wait_recv()

                @pl.when(up if way == 0 else down)
                def _():
                    for copy in copies:
                        copy.start()

                arrived0(piece)

    def chain_piece(k, way):
        return 8 - k + z if way == 0 else k - 8 + z

    def chain_step(k):
        for way in (0, 1):
            piece = chain_piece(k, way)

            @pl.when(jnp.logical_and(piece >= 0, piece < NZ))
            def _():
                copies = chain(piece, way)
                for copy in copies:
                    copy.wait_recv()

                @pl.when(up if way == 0 else down)
                def _():
                    for copy in copies:
                        copy.start()

                along_x1(piece, way, 0).start()
                along_x1(piece, way, 1).start()

    def x_piece0(piece):
        for way in (0, 1):
            came_x0(piece, way).wait_recv()
            onward(rv0, s_h0, r_h0, piece, way).start()

    def x_step(k):
        @pl.when(k == 0)
        def _():
            x_piece0(z)

        for way in (0, 1):
            piece = z - k if way == 0 else z + k

            @pl.when(jnp.logical_and(k > 0, piece >= 0 if way == 0 else piece < NZ))
            def _():
                x_piece0(piece)

            behind = chain_piece(k, way)

            @pl.when(jnp.logical_and(behind >= 0, behind < NZ))
            def _():
                came_x1(behind, way, way).wait_recv()
                onward(rv1, s_h1, r_h1, behind, way).start()

    def cross_at(k):
        for u in range(4):
            if isinstance(k, int):
                if CROSS_AT[u] == k:
                    cross(u).start()
            elif CROSS_AT[u] > 0:

                @pl.when(k == CROSS_AT[u])
                def _():
                    cross(u).start()

    @pl.when(source)
    def _():
        for copy in keep():
            copy.start()
        for step in (1, 2, 3):
            for copy in scatter(step):
                copy.start()

    for steps in range(1, 6):
        send_meta(steps).start()
    cross_at(0)
    send_y().start()

    @pl.when(kap == 1)
    def _():
        send_own().start()

    for rv in (rv0, rv1):
        rv[ZERO] = jnp.zeros((BS, BS), jnp.bfloat16)
    own_meta = pltpu.make_async_copy(meta, ml.at[0], local.at[2])
    own_meta.start()

    @pl.when(source)
    def _():
        for copy in keep():
            copy.wait()

    @pl.when(jnp.logical_not(source))
    def _():
        part = quarter(rv0, z, x)
        remote(part, part, s_sc.at[0], r_sc.at[0], (r, sib)).wait_recv()
        remote(m0.at[z], m0.at[z], s_scm.at[0], r_sc.at[1], (r, sib)).wait_recv()

    @pl.when(up)
    def _():
        for copy in along_z(z, 0):
            copy.start()

    @pl.when(down)
    def _():
        for copy in along_z(z, 1):
            copy.start()

    arrived0(z)

    @pl.loop(1, 16 + LAG)
    def _(k):
        z_step(k)
        chain_step(k)
        x_step(k - LAG)
        cross_at(k)

        @pl.when(k == 8)
        def _():
            send_y().wait_recv()
            pass_y().start()

    for u in range(4):
        cross(u).wait_recv()
    pass_cross().start()

    @pl.when(kap == 0)
    def _():
        pass_cross_y().start()

    @pl.loop(0, NZ)
    def _(piece):
        for way in (0, 1):
            came_onward(rv0, s_h0, r_h0, piece, way).wait_recv()

    own_meta.wait()
    for steps in range(1, 6):
        send_meta(steps).wait_recv()
    tables = [
        pltpu.make_async_copy(ml, tl, local.at[3]),
        pltpu.make_async_copy(m0, t0, local.at[4]),
        pltpu.make_async_copy(m1, t1, local.at[5]),
    ]
    for copy in tables:
        copy.start()
    for copy in tables:
        copy.wait()
    came_left(0).wait_recv()
    came_left(2).wait_recv()


    def picks(tile, section, inner, kept):
        group = (2 * c + 4 * tile + 2 * section + (inner >> 3)) % NZ
        table = t1 if tile else t0
        row = 2 * (inner & 7)
        first, second = table[group, 0, row], table[group, 0, row + 1]
        base = group * 16 + row
        return [
            jnp.where(first == wanted, base, jnp.where(second == wanted, base + 1, ZERO)) for wanted in kept
        ]

    def kept_of(section, a):
        return [tl[section, 0, 16 + 4 * a + t] for t in range(4)]

    def terms(total, lefts, rv, spots):
        lhs = jnp.concatenate(lefts, axis=1)
        parts = []
        for pair in (0, 2):
            rhs = jnp.concatenate(
                [jnp.concatenate([rv[spot[pair]], rv[spot[pair + 1]]], axis=1) for spot in spots], axis=0
            )
            parts.append(jnp.dot(lhs, rhs, preferred_element_type=jnp.float32))
        return parts if total is None else [old + new for old, new in zip(total, parts)]

    def send_square(tile, a):
        slot = jnp.where(kap == 0, 3 - 2 * tile, 1 + 2 * tile)
        to = sib if tile == 1 else jnp.where(kap == 0, back(3), sib)
        rows = pl.ds(4 * a, 4)
        return remote(sv.at[2 * tile, rows], sv.at[slot, rows], s_sq.at[tile, a], r_sq.at[slot, a], (r, to))

    def came_square(slot, a):
        rows = pl.ds(4 * a, 4)
        return remote(sv.at[slot, rows], sv.at[slot, rows], s_sq.at[0, a], r_sq.at[slot, a], (r, sib))

    def square(tile, a):
        kept = kept_of(2 * tile, a)
        total = None
        for section in range(4):
            place = 2 * tile + section
            spots = [picks(tile, section, tl[place, 0, 2 * a + i], kept) for i in range(2)]
            lefts = [d[2 * a + i] if place == 0 else left[place - 1, 2 * a + i] for i in range(2)]
            total = terms(total, lefts, rv1 if tile else rv0, spots)
        for t in range(4):
            sv[2 * tile, 4 * a + t] = total[t // 2][:, (t % 2) * BS : (t % 2 + 1) * BS].astype(jnp.bfloat16)
        send_square(tile, a).start()

    def cube(sections, a, total):
        kept = kept_of(0, a)
        for section in sections:
            inner = kept_of(section, a)
            for i in (0, 2):
                spots = [picks(0, section, inner[i + e], kept) for e in range(2)]
                total = terms(total, [sv[section, 4 * a + i + e] for e in range(2)], rv0, spots)
        return total

    @pl.loop(0, 8)
    def _(a):
        square(0, a)

    @pl.loop(0, NZ)
    def _(piece):
        for way in (0, 1):
            came_x1(piece, way, 1 - way).wait_recv()
            came_onward(rv1, s_h1, r_h1, piece, way).wait_recv()

    came_left(4).wait_recv()

    @pl.loop(0, 8)
    def _(a):
        square(1, a)

    @pl.loop(0, 8)
    def _(a):
        total = cube((0, 2), a, None)
        acc[a, 0] = total[0]
        acc[a, 1] = total[1]

    @pl.loop(0, 8)
    def _(a):
        came_square(1, a).wait_recv()
        came_square(3, a).wait_recv()
        total = cube((1, 3), a, [acc[a, 0], acc[a, 1]])
        for t in range(4):
            part = total[t // 2][:, (t % 2) * BS : (t % 2 + 1) * BS]
            out[4 * a + t] = (3.0 * sv[0, 4 * a + t].astype(jnp.float32) - 2.0 * part).astype(jnp.bfloat16)


    @pl.loop(0, NZ)
    def _(piece):
        for way in (0, 1):
            along_x0(piece, way).wait_send()
            onward(rv0, s_h0, r_h0, piece, way).wait_send()
            along_x1(piece, 0, way).wait_send()
            along_x1(piece, 1, way).wait_send()
            onward(rv1, s_h1, r_h1, piece, way).wait_send()
            for copy in chain(piece, way):
                copy.wait_send()

            @pl.when(jnp.logical_and(up, piece <= z) if way == 0 else jnp.logical_and(down, piece >= z))
            def _():
                for copy in along_z(piece, way):
                    copy.wait_send()

        send_square(0, piece).wait_send()
        send_square(1, piece).wait_send()

    for u in range(4):
        cross(u).wait_send()
    for steps in range(1, 6):
        send_meta(steps).wait_send()

    @pl.when(source)
    def _():
        for step in (1, 2, 3):
            for copy in scatter(step):
                copy.wait_send()

    send_y().wait_send()
    pass_cross().wait_send()
    pass_y().wait_send()

    @pl.when(kap == 1)
    def _():
        send_own().wait_send()

    @pl.when(kap == 0)
    def _():
        pass_cross_y().wait_send()


def on_device(density, pattern, kept_pattern):
    own = density.reshape(16, BS, BS)
    meta = jnp.concatenate([pattern.reshape(16), kept_pattern.reshape(32)])
    meta = jnp.pad(meta, (0, 8 * BS - 48)).reshape(8, BS)
    dma = pltpu.SemaphoreType.DMA
    vmem = pl.BlockSpec(memory_space=pltpu.VMEM)
    blocks = lambda *shape: pltpu.VMEM(shape + (BS, BS), jnp.bfloat16)
    table = lambda space, count: space((count, 8, BS), jnp.int32)
    out = pl.pallas_call(
        kernel,
        out_shape=jax.ShapeDtypeStruct((32, BS, BS), jnp.bfloat16),
        in_specs=[vmem, vmem],
        out_specs=vmem,
        scratch_shapes=[
            blocks(5, 16),
            blocks(ZERO + 1),
            blocks(ZERO + 1),
            blocks(4, 32),
            pltpu.VMEM((8, 2, BS, 2 * BS), jnp.float32),
            table(pltpu.VMEM, 6),
            table(pltpu.VMEM, NZ),
            table(pltpu.VMEM, NZ),
            table(pltpu.SMEM, 6),
            table(pltpu.SMEM, NZ),
            table(pltpu.SMEM, NZ),
            dma((3,)),
            dma((3,)),
            dma((2,)),
            dma((6,)),
            dma((NZ, 2)),
            dma((NZ,)),
            dma((NZ, 2)),
            dma((NZ,)),
            dma((NZ,)),
            dma((NZ,)),
            dma((NZ,)),
            dma((NZ,)),
            dma((NZ,)),
            dma((NZ,)),
            dma((NZ, 2)),
            dma((NZ, 2)),
            dma((NZ, 2)),
            dma((NZ, 2)),
            dma((NZ, 2, 2)),
            dma((NZ, 2, 2)),
            dma((NZ, 2)),
            dma((NZ, 2)),
            dma((4,)),
            dma((4,)),
            dma((5,)),
            dma((5,)),
            dma((5,)),
            dma((5,)),
            dma((2, 8)),
            dma((4, 8)),
        ],
        compiler_params=pltpu.CompilerParams(
            collective_id=0, has_side_effects=True, vmem_limit_bytes=40 << 20
        ),
        cost_estimate=pl.CostEstimate(flops=4 << 30, bytes_accessed=12 << 20, transcendentals=0),
        name="purify",
    )(meta, own)
    return out.reshape(8, 1, 4, BS, BS)


def solution(mesh):
    in_specs = (P("row", "col", None, None, None), P("row", "col", None), P("row", "col", None))
    out_specs = P("row", "col", None, None, None)
    return jax.shard_map(
        on_device, mesh=mesh, in_specs=in_specs, out_specs=out_specs, check_vma=False
    )
```

```python
import jax
import jax.numpy as jnp
from jax import lax
from jax.experimental import pallas as pl
from jax.experimental.pallas import tpu as pltpu
from jax.sharding import PartitionSpec as P

MESH = pl.DeviceIdType.MESH
ROWS, COLS = 32, 16
NX, NZ = 4, 8
BS = 128
ZERO = 128
LAG = 2
BEHIND = 1
STEPS = 7 + BEHIND + LAG
CROSS_AT = (0, 6, 8, 10)


def remote(src, dst, send, recv, device):
    return pltpu.make_async_remote_copy(
        src_ref=src, dst_ref=dst, send_sem=send, recv_sem=recv, device_id=device, device_id_type=MESH
    )


def kernel(
    meta, held, out,
    d, left, rv0, rv1, sv, acc, ml, m0, m1, tl, t0, t1,
    s_sc, s_scm, r_sc, local,
    s_z, r_z, s_zm, r_zm,
    s_i, s_im, s_c, r_c, s_cm, r_cm,
    s_x0, r_x0, s_h0, r_h0, s_x1, r_x1, s_h1, r_h1,
    s_cr, r_cr, s_pc, r_pc, s_py, r_py, s_l, r_l, s_ml, r_ml, s_sq, r_sq,
):
    r, c = lax.axis_index("row"), lax.axis_index("col")
    x, z, kap = r // NZ, r % NZ, c % 2
    sib = c + 1 - 2 * kap
    xr, xl, xo = (x + 1) % NX, (x + 3) % NX, (x + 2) % NX
    up, down = z < NZ - 1, z > 0
    deep = z % 4
    source = (r - 2 * c + ROWS) % ROWS < NZ
    top, bottom = jnp.logical_not(up), jnp.logical_not(down)
    middle = jnp.logical_or(z == 3, z == 4)
    bands = (
        (rv0, m0, s_x0, r_x0, s_h0, r_h0),
        (rv1, m1, s_x1, r_x1, s_h1, r_h1),
    )

    def back(steps):
        return (c + COLS - steps) % COLS

    def ahead(steps):
        return (c + steps) % COLS

    own = pltpu.make_async_copy(held, d, local.at[6])
    own.start()
    for rv in (rv0, rv1):
        rv[ZERO] = jnp.zeros((BS, BS), jnp.bfloat16)
    barrier = pltpu.get_barrier_semaphore()

    def greet(device):
        pl.semaphore_signal(barrier, inc=1, device_id=device, device_id_type=MESH)

    for steps in range(1, 6):
        greet((r, back(steps)))
        greet((r, ahead(steps)))
    for other in (xr, xl, xo):
        greet((other * NZ + z, c))

    @pl.when(up)
    def _():
        greet((r + 1, c))

    @pl.when(down)
    def _():
        greet((r - 1, c))

    @pl.when(top)
    def _():
        greet((r - 7, back(2)))
        greet((r - 3, back(2)))
        greet((r - 7, ahead(2)))

    @pl.when(bottom)
    def _():
        greet((r + 7, back(2)))
        greet((r + 3, back(2)))
        greet((r + 7, ahead(2)))

    @pl.when(z == 4)
    def _():
        greet((r + 3, ahead(2)))

    @pl.when(z == 3)
    def _():
        greet((r - 3, ahead(2)))

    ends = jnp.logical_or(top, bottom)
    pl.semaphore_wait(barrier, jnp.where(ends, 17, jnp.where(middle, 16, 15)))
    own.wait()


    def quarter(buffer, piece, which, start=0, size=4):
        return buffer.at[pl.ds(piece * 16 + 4 * which + start, size)]

    def scatter(step):
        other = (x + step) % NX
        to = (other * NZ + z, c)
        return (
            remote(d.at[pl.ds(4 * other, 4)], quarter(rv0, z, other), s_sc.at[step - 1], r_sc.at[0], to),
            remote(meta, m0.at[z], s_scm.at[step - 1], r_sc.at[1], to),
        )

    def keep():
        return (
            pltpu.make_async_copy(d.at[pl.ds(4 * x, 4)], quarter(rv0, z, x), local.at[0]),
            pltpu.make_async_copy(meta, m0.at[z], local.at[1]),
        )

    def along_z(piece, half, way):
        part = quarter(rv0, piece, x, 2 * half, 2)
        to = (r + 1 if way == 0 else r - 1, c)
        copies = [remote(part, part, s_z.at[piece, half, way], r_z.at[piece, half], to)]
        if half == 0:
            copies.append(remote(m0.at[piece], m0.at[piece], s_zm.at[piece, way], r_zm.at[piece], to))
        return copies

    def chain(piece, half, way):
        part = quarter(rv1, piece, x, 2 * half, 2)
        to = (r + 1 if way == 0 else r - 1, c)
        copies = [remote(part, part, s_c.at[piece, half], r_c.at[piece, half], to)]
        if half == 0:
            copies.append(remote(m1.at[piece], m1.at[piece], s_cm.at[piece], r_cm.at[piece], to))
        return copies

    def inject(piece, half, way):
        copies = []
        for entry in (0, 1):
            distance = (7, 3)[entry]
            to = (r - distance if way == 0 else r + distance, back(2))
            copies.append(
                remote(
                    quarter(rv0, piece, x, 2 * half, 2),
                    quarter(rv1, piece, x, 2 * half, 2),
                    s_i.at[piece, half, entry],
                    r_c.at[piece, half],
                    to,
                )
            )
            if half == 0:
                copies.append(remote(m0.at[piece], m1.at[piece], s_im.at[piece, entry], r_cm.at[piece], to))
        return copies

    def ring(way):
        return ((xr if way == 0 else xl) * NZ + z, c)

    def along_x(tile, piece, half, way):
        rv, _, send, recv, _, _ = bands[tile]
        part = quarter(rv, piece, x, 2 * half, 2)
        return remote(part, part, send.at[piece, half, way], recv.at[piece, half, way], ring(way))

    def came_x(tile, piece, half, way):
        rv, _, send, recv, _, _ = bands[tile]
        part = quarter(rv, piece, xl if way == 0 else xr, 2 * half, 2)
        return remote(part, part, send.at[piece, half, way], recv.at[piece, half, way], ring(way))

    def onward(tile, piece, way):
        rv, _, _, _, send, recv = bands[tile]
        part = quarter(rv, piece, xl if way == 0 else xr, 2 * way, 2)
        return remote(part, part, send.at[piece, way], recv.at[piece, way], ring(way))

    def came_onward(tile, piece, way):
        rv, _, _, _, send, recv = bands[tile]
        part = quarter(rv, piece, xo, 2 * way, 2)
        return remote(part, part, send.at[piece, way], recv.at[piece, way], ring(way))

    def cross(u):
        part = pl.ds(4 * u, 4)
        return remote(d.at[part], left.at[1, part], s_cr.at[u], r_cr.at[u], (r, back(2)))

    def pass_cross(u):
        part = pl.ds(4 * u, 4)
        return remote(left.at[1, part], left.at[2 * kap, part], s_pc.at[u], r_pc.at[u], (r, sib))

    def came_pass(u):
        part = left.at[2 - 2 * kap, pl.ds(4 * u, 4)]
        return remote(part, part, s_pc.at[u], r_pc.at[u], (r, sib))

    def pass_cross_y(u):
        part = pl.ds(4 * u, 4)
        return remote(left.at[1, part], left.at[4, part], s_py.at[u], r_py.at[u], (r, back(3)))

    def send_y():
        return remote(d, left.at[3], s_l.at[0], r_l.at[0], (r, back(4)))

    def send_own():
        return remote(d, left.at[0], s_l.at[1], r_l.at[1], (r, sib))

    def pass_y():
        return remote(left.at[3], left.at[2 + 2 * kap], s_l.at[2], r_l.at[2], (r, sib))

    def came_y():
        part = left.at[4 - 2 * kap]
        return remote(part, part, s_l.at[2], r_l.at[2], (r, sib))

    def send_meta(steps):
        return remote(meta, ml.at[steps], s_ml.at[steps - 1], r_ml.at[steps - 1], (r, back(steps)))


    def arrived0(piece, half):
        along_x(0, piece, half, 0).start()
        along_x(0, piece, half, 1).start()

        @pl.when(jnp.logical_and(top, piece >= 4))
        def _():
            for copy in inject(piece, half, 0):
                copy.start()

        @pl.when(jnp.logical_and(bottom, piece < 4))
        def _():
            for copy in inject(piece, half, 1):
                copy.start()

    def z_step(k):
        for way in (0, 1):
            piece = z - k if way == 0 else z + k

            @pl.when(piece >= 0 if way == 0 else piece < NZ)
            def _():
                for half in (0, 1):
                    copies = along_z(piece, half, way)
                    for copy in copies:
                        copy.wait_recv()

                    @pl.when(up if way == 0 else down)
                    def _():
                        for copy in copies:
                            copy.start()

                    arrived0(piece, half)

    def chain_order(k, way):
        return k - 1 - BEHIND - (deep if way == 0 else 3 - deep)

    def chain_on(way):
        return deep < 3 if way == 0 else deep > 0

    def chain_step(k):
        for way in (0, 1):
            order = chain_order(k, way)
            piece = 7 - order if way == 0 else order

            @pl.when(jnp.logical_and(order >= 0, order < 4))
            def _():
                for half in (0, 1):
                    copies = chain(piece, half, way)
                    for copy in copies:
                        copy.wait_recv()

                    @pl.when(chain_on(way))
                    def _():
                        for copy in copies:
                            copy.start()

                    along_x(1, piece, half, 0).start()
                    along_x(1, piece, half, 1).start()

    def x_piece(tile, piece):
        for way in (0, 1):
            came_x(tile, piece, way, way).wait_recv()
            onward(tile, piece, way).start()

    def x_step(k):
        @pl.when(k == 0)
        def _():
            x_piece(0, z)

        for way in (0, 1):
            piece = z - k if way == 0 else z + k

            @pl.when(jnp.logical_and(k > 0, piece >= 0 if way == 0 else piece < NZ))
            def _():
                x_piece(0, piece)

        for way in (0, 1):
            order = chain_order(k, way)

            @pl.when(jnp.logical_and(order >= 0, order < 4))
            def _():
                x_piece(1, 7 - order if way == 0 else order)

    @pl.when(source)
    def _():
        for copy in keep():
            copy.start()
        for step in (1, 2, 3):
            for copy in scatter(step):
                copy.start()

    for steps in range(1, 6):
        send_meta(steps).start()
    for u in range(4):
        if CROSS_AT[u] == 0:
            cross(u).start()
    send_y().start()

    @pl.when(kap == 1)
    def _():
        send_own().start()

    own_meta = pltpu.make_async_copy(meta, ml.at[0], local.at[2])
    own_meta.start()

    @pl.when(source)
    def _():
        for copy in keep():
            copy.wait()

    @pl.when(jnp.logical_not(source))
    def _():
        part = quarter(rv0, z, x)
        remote(part, part, s_sc.at[0], r_sc.at[0], (r, sib)).wait_recv()
        remote(m0.at[z], m0.at[z], s_scm.at[0], r_sc.at[1], (r, sib)).wait_recv()

    for half in (0, 1):

        @pl.when(up)
        def _():
            for copy in along_z(z, half, 0):
                copy.start()

        @pl.when(down)
        def _():
            for copy in along_z(z, half, 1):
                copy.start()

        arrived0(z, half)

    @pl.loop(1, STEPS + 1)
    def _(k):
        z_step(k)
        chain_step(k)
        x_step(k - LAG)
        for u in range(4):
            if CROSS_AT[u] > 0:

                @pl.when(k == CROSS_AT[u])
                def _():
                    cross(u).start()

        @pl.when(k == 6)
        def _():
            send_y().wait_recv()
            pass_y().start()

    own_meta.wait()
    for steps in range(1, 6):
        send_meta(steps).wait_recv()
    tables = [
        pltpu.make_async_copy(ml, tl, local.at[3]),
        pltpu.make_async_copy(m0, t0, local.at[4]),
        pltpu.make_async_copy(m1, t1, local.at[5]),
    ]
    for copy in tables:
        copy.start()

    @pl.loop(0, NZ)
    def _(piece):
        for way in (0, 1):
            came_x(0, piece, way, 1 - way).wait_recv()
            came_onward(0, piece, way).wait_recv()

    for copy in tables:
        copy.wait()

    @pl.when(kap == 0)
    def _():
        send_own().wait_recv()

    came_y().wait_recv()


    def picks(tile, section, inner, kept):
        group = (2 * c + 4 * tile + 2 * section + (inner >> 3)) % NZ
        table = t1 if tile else t0
        row = 2 * (inner & 7)
        first, second = table[group, 0, row], table[group, 0, row + 1]
        base = group * 16 + row
        return [
            jnp.where(first == wanted, base, jnp.where(second == wanted, base + 1, ZERO)) for wanted in kept
        ]

    def kept_of(section, a):
        return [tl[section, 0, 16 + 4 * a + t] for t in range(4)]

    def terms(total, lefts, rv, spots):
        lhs = jnp.concatenate(lefts, axis=1)
        parts = []
        for pair in (0, 2):
            rhs = jnp.concatenate(
                [jnp.concatenate([rv[spot[pair]], rv[spot[pair + 1]]], axis=1) for spot in spots], axis=0
            )
            parts.append(jnp.dot(lhs, rhs, preferred_element_type=jnp.float32))
        return parts if total is None else [old + new for old, new in zip(total, parts)]

    def send_square(tile, a):
        slot = jnp.where(kap == 0, 3 - 2 * tile, 1 + 2 * tile)
        to = sib if tile == 1 else jnp.where(kap == 0, back(3), sib)
        rows = pl.ds(4 * a, 4)
        return remote(sv.at[2 * tile, rows], sv.at[slot, rows], s_sq.at[tile, a], r_sq.at[slot, a], (r, to))

    def came_square(slot, a):
        rows = pl.ds(4 * a, 4)
        return remote(sv.at[slot, rows], sv.at[slot, rows], s_sq.at[0, a], r_sq.at[slot, a], (r, sib))

    def square(tile, a):
        kept = kept_of(2 * tile, a)
        total = None
        for section in range(4):
            place = 2 * tile + section
            spots = [picks(tile, section, tl[place, 0, 2 * a + i], kept) for i in range(2)]
            lefts = [d[2 * a + i] if place == 0 else left[place - 1, 2 * a + i] for i in range(2)]
            total = terms(total, lefts, rv1 if tile else rv0, spots)
        for t in range(4):
            sv[2 * tile, 4 * a + t] = total[t // 2][:, (t % 2) * BS : (t % 2 + 1) * BS].astype(jnp.bfloat16)
        send_square(tile, a).start()

    def cube(sections, a, total):
        kept = kept_of(0, a)
        for section in sections:
            inner = kept_of(section, a)
            for i in (0, 2):
                spots = [picks(0, section, inner[i + e], kept) for e in range(2)]
                total = terms(total, [sv[section, 4 * a + i + e] for e in range(2)], rv0, spots)
        return total

    def keep_total(a, total):
        acc[a, 0] = total[0]
        acc[a, 1] = total[1]

    @pl.loop(0, 4)
    def _(u):
        cross(u).wait_recv()
        pass_cross(u).start()

        @pl.when(kap == 0)
        def _():
            pass_cross_y(u).start()

        came_pass(u).wait_recv()
        for a in (2 * u, 2 * u + 1):
            square(0, a)
        for a in (2 * u, 2 * u + 1):
            keep_total(a, cube((0,), a, None))

    @pl.loop(0, NZ)
    def _(piece):
        for way in (0, 1):
            came_x(1, piece, way, 1 - way).wait_recv()
            came_onward(1, piece, way).wait_recv()

    @pl.loop(0, 4)
    def _(u):
        @pl.when(kap == 1)
        def _():
            pass_cross_y(u).wait_recv()

        for a in (2 * u, 2 * u + 1):
            square(1, a)

    @pl.loop(0, 8)
    def _(a):
        keep_total(a, cube((2,), a, [acc[a, 0], acc[a, 1]]))


    @pl.loop(0, NZ)
    def _(piece):
        for way in (0, 1):
            for tile in (0, 1):
                along_x(tile, piece, 0, way).wait_send()
                along_x(tile, piece, 1, way).wait_send()
                onward(tile, piece, way).wait_send()

            @pl.when(jnp.logical_and(up, piece <= z) if way == 0 else jnp.logical_and(down, piece >= z))
            def _():
                for half in (0, 1):
                    for copy in along_z(piece, half, way):
                        copy.wait_send()

            mine = piece >= 4 if way == 0 else piece < 4

            @pl.when(jnp.logical_and(chain_on(way), mine))
            def _():
                for half in (0, 1):
                    for copy in chain(piece, half, way):
                        copy.wait_send()

            @pl.when(jnp.logical_and(top if way == 0 else bottom, mine))
            def _():
                for half in (0, 1):
                    for copy in inject(piece, half, way):
                        copy.wait_send()

    for u in range(4):
        cross(u).wait_send()
        pass_cross(u).wait_send()
    for steps in range(1, 6):
        send_meta(steps).wait_send()

    @pl.when(source)
    def _():
        for step in (1, 2, 3):
            for copy in scatter(step):
                copy.wait_send()

    send_y().wait_send()
    pass_y().wait_send()

    @pl.when(kap == 1)
    def _():
        send_own().wait_send()

    @pl.when(kap == 0)
    def _():
        for u in range(4):
            pass_cross_y(u).wait_send()

    @pl.loop(0, 8)
    def _(a):
        came_square(1, a).wait_recv()
        came_square(3, a).wait_recv()
        total = cube((1, 3), a, [acc[a, 0], acc[a, 1]])
        for t in range(4):
            part = total[t // 2][:, (t % 2) * BS : (t % 2 + 1) * BS]
            out[4 * a + t] = (3.0 * sv[0, 4 * a + t].astype(jnp.float32) - 2.0 * part).astype(jnp.bfloat16)
        send_square(0, a).wait_send()
        send_square(1, a).wait_send()


def on_device(density, pattern, kept_pattern):
    own = density.reshape(16, BS, BS)
    meta = jnp.concatenate([pattern.reshape(16), kept_pattern.reshape(32)])
    meta = jnp.pad(meta, (0, 8 * BS - 48)).reshape(8, BS)
    dma = pltpu.SemaphoreType.DMA
    vmem = pl.BlockSpec(memory_space=pltpu.VMEM)
    blocks = lambda *shape: pltpu.VMEM(shape + (BS, BS), jnp.bfloat16)
    table = lambda space, count: space((count, 8, BS), jnp.int32)
    out = pl.pallas_call(
        kernel,
        out_shape=jax.ShapeDtypeStruct((32, BS, BS), jnp.bfloat16),
        in_specs=[vmem, pl.BlockSpec(memory_space=pl.ANY)],
        out_specs=vmem,
        scratch_shapes=[
            blocks(16),
            blocks(5, 16),
            blocks(ZERO + 1),
            blocks(ZERO + 1),
            blocks(4, 32),
            pltpu.VMEM((8, 2, BS, 2 * BS), jnp.float32),
            table(pltpu.VMEM, 6),
            table(pltpu.VMEM, NZ),
            table(pltpu.VMEM, NZ),
            table(pltpu.SMEM, 6),
            table(pltpu.SMEM, NZ),
            table(pltpu.SMEM, NZ),
            dma((3,)),
            dma((3,)),
            dma((2,)),
            dma((7,)),
            dma((NZ, 2, 2)),
            dma((NZ, 2)),
            dma((NZ, 2)),
            dma((NZ,)),
            dma((NZ, 2, 2)),
            dma((NZ, 2)),
            dma((NZ, 2)),
            dma((NZ, 2)),
            dma((NZ,)),
            dma((NZ,)),
            dma((NZ, 2, 2)),
            dma((NZ, 2, 2)),
            dma((NZ, 2)),
            dma((NZ, 2)),
            dma((NZ, 2, 2)),
            dma((NZ, 2, 2)),
            dma((NZ, 2)),
            dma((NZ, 2)),
            dma((4,)),
            dma((4,)),
            dma((4,)),
            dma((4,)),
            dma((4,)),
            dma((4,)),
            dma((3,)),
            dma((3,)),
            dma((5,)),
            dma((5,)),
            dma((2, 8)),
            dma((4, 8)),
        ],
        compiler_params=pltpu.CompilerParams(
            collective_id=0, has_side_effects=True, vmem_limit_bytes=40 << 20
        ),
        cost_estimate=pl.CostEstimate(flops=4 << 30, bytes_accessed=12 << 20, transcendentals=0),
        name="purify",
    )(meta, own)
    return out.reshape(8, 1, 4, BS, BS)


def solution(mesh):
    in_specs = (P("row", "col", None, None, None), P("row", "col", None), P("row", "col", None))
    out_specs = P("row", "col", None, None, None)
    return jax.shard_map(
        on_device, mesh=mesh, in_specs=in_specs, out_specs=out_specs, check_vma=False
    )
```

```python
import jax
import jax.numpy as jnp
from jax import lax
from jax.experimental import pallas as pl
from jax.experimental.pallas import tpu as pltpu
from jax.sharding import PartitionSpec as P

MESH = pl.DeviceIdType.MESH
ROWS, COLS = 32, 16
NX, NZ = 4, 8
BS = 128
ZERO = 128
LAG = 2
BEHIND = 1
STEPS = 7 + BEHIND + LAG
CROSS_AT = (0, 6, 8, 10)


def remote(src, dst, send, recv, device):
    return pltpu.make_async_remote_copy(
        src_ref=src, dst_ref=dst, send_sem=send, recv_sem=recv, device_id=device, device_id_type=MESH
    )


def kernel(
    pattern, kept_pattern, held, out,
    meta, d, left, rv0, rv1, sv, acc, ml, m0, m1, tl, t0, t1,
    s_sc, s_scm, r_sc, local,
    s_z, r_z, s_zm, r_zm,
    s_i, s_im, s_c, r_c, s_cm, r_cm,
    s_x0, r_x0, s_h0, r_h0, s_x1, r_x1, s_h1, r_h1,
    s_cr, r_cr, s_pc, r_pc, s_py, r_py, s_l, r_l, s_ml, r_ml, s_sq, r_sq,
):
    r, c = lax.axis_index("row"), lax.axis_index("col")
    x, z, kap = r // NZ, r % NZ, c % 2
    sib = c + 1 - 2 * kap
    xr, xl, xo = (x + 1) % NX, (x + 3) % NX, (x + 2) % NX
    up, down = z < NZ - 1, z > 0
    deep = z % 4
    source = (r - 2 * c + ROWS) % ROWS < NZ
    top, bottom = jnp.logical_not(up), jnp.logical_not(down)
    middle = jnp.logical_or(z == 3, z == 4)
    bands = (
        (rv0, m0, s_x0, r_x0, s_h0, r_h0),
        (rv1, m1, s_x1, r_x1, s_h1, r_h1),
    )

    def back(steps):
        return (c + COLS - steps) % COLS

    def ahead(steps):
        return (c + steps) % COLS

    own = pltpu.make_async_copy(held, d, local.at[6])
    own.start()
    meta[...] = jnp.zeros_like(meta)
    meta[0:2, 0:8] = pattern[...]
    meta[2:6, 0:8] = kept_pattern[...]
    for rv in (rv0, rv1):
        rv[ZERO] = jnp.zeros((BS, BS), jnp.bfloat16)
    barrier = pltpu.get_barrier_semaphore()

    def greet(device):
        pl.semaphore_signal(barrier, inc=1, device_id=device, device_id_type=MESH)

    for steps in range(1, 6):
        greet((r, back(steps)))
        greet((r, ahead(steps)))
    for other in (xr, xl, xo):
        greet((other * NZ + z, c))

    @pl.when(up)
    def _():
        greet((r + 1, c))

    @pl.when(down)
    def _():
        greet((r - 1, c))

    @pl.when(top)
    def _():
        greet((r - 7, back(2)))
        greet((r - 3, back(2)))
        greet((r - 7, ahead(2)))

    @pl.when(bottom)
    def _():
        greet((r + 7, back(2)))
        greet((r + 3, back(2)))
        greet((r + 7, ahead(2)))

    @pl.when(z == 4)
    def _():
        greet((r + 3, ahead(2)))

    @pl.when(z == 3)
    def _():
        greet((r - 3, ahead(2)))

    ends = jnp.logical_or(top, bottom)
    pl.semaphore_wait(barrier, jnp.where(ends, 17, jnp.where(middle, 16, 15)))
    own.wait()


    def quarter(buffer, piece, which, start=0, size=4):
        return buffer.at[pl.ds(piece * 16 + 4 * which + start, size)]

    def scatter(step):
        other = (x + step) % NX
        to = (other * NZ + z, c)
        return (
            remote(d.at[pl.ds(4 * other, 4)], quarter(rv0, z, other), s_sc.at[step - 1], r_sc.at[0], to),
            remote(meta, m0.at[z], s_scm.at[step - 1], r_sc.at[1], to),
        )

    def keep():
        return (
            pltpu.make_async_copy(d.at[pl.ds(4 * x, 4)], quarter(rv0, z, x), local.at[0]),
            pltpu.make_async_copy(meta, m0.at[z], local.at[1]),
        )

    def along_z(piece, half, way):
        part = quarter(rv0, piece, x, 2 * half, 2)
        to = (r + 1 if way == 0 else r - 1, c)
        copies = [remote(part, part, s_z.at[piece, half, way], r_z.at[piece, half], to)]
        if half == 0:
            copies.append(remote(m0.at[piece], m0.at[piece], s_zm.at[piece, way], r_zm.at[piece], to))
        return copies

    def chain(piece, half, way):
        part = quarter(rv1, piece, x, 2 * half, 2)
        to = (r + 1 if way == 0 else r - 1, c)
        copies = [remote(part, part, s_c.at[piece, half], r_c.at[piece, half], to)]
        if half == 0:
            copies.append(remote(m1.at[piece], m1.at[piece], s_cm.at[piece], r_cm.at[piece], to))
        return copies

    def inject(piece, half, way):
        copies = []
        for entry in (0, 1):
            distance = (7, 3)[entry]
            to = (r - distance if way == 0 else r + distance, back(2))
            copies.append(
                remote(
                    quarter(rv0, piece, x, 2 * half, 2),
                    quarter(rv1, piece, x, 2 * half, 2),
                    s_i.at[piece, half, entry],
                    r_c.at[piece, half],
                    to,
                )
            )
            if half == 0:
                copies.append(remote(m0.at[piece], m1.at[piece], s_im.at[piece, entry], r_cm.at[piece], to))
        return copies

    def ring(way):
        return ((xr if way == 0 else xl) * NZ + z, c)

    def along_x(tile, piece, half, way):
        rv, _, send, recv, _, _ = bands[tile]
        part = quarter(rv, piece, x, 2 * half, 2)
        return remote(part, part, send.at[piece, half, way], recv.at[piece, half, way], ring(way))

    def came_x(tile, piece, half, way):
        rv, _, send, recv, _, _ = bands[tile]
        part = quarter(rv, piece, xl if way == 0 else xr, 2 * half, 2)
        return remote(part, part, send.at[piece, half, way], recv.at[piece, half, way], ring(way))

    def onward(tile, piece, way):
        rv, _, _, _, send, recv = bands[tile]
        part = quarter(rv, piece, xl if way == 0 else xr, 2 * way, 2)
        return remote(part, part, send.at[piece, way], recv.at[piece, way], ring(way))

    def came_onward(tile, piece, way):
        rv, _, _, _, send, recv = bands[tile]
        part = quarter(rv, piece, xo, 2 * way, 2)
        return remote(part, part, send.at[piece, way], recv.at[piece, way], ring(way))

    def cross(u):
        part = pl.ds(4 * u, 4)
        return remote(d.at[part], left.at[1, part], s_cr.at[u], r_cr.at[u], (r, back(2)))

    def pass_cross(u):
        part = pl.ds(4 * u, 4)
        return remote(left.at[1, part], left.at[2 * kap, part], s_pc.at[u], r_pc.at[u], (r, sib))

    def came_pass(u):
        part = left.at[2 - 2 * kap, pl.ds(4 * u, 4)]
        return remote(part, part, s_pc.at[u], r_pc.at[u], (r, sib))

    def pass_cross_y(u):
        part = pl.ds(4 * u, 4)
        return remote(left.at[1, part], left.at[4, part], s_py.at[u], r_py.at[u], (r, back(3)))

    def send_y():
        return remote(d, left.at[3], s_l.at[0], r_l.at[0], (r, back(4)))

    def send_own():
        return remote(d, left.at[0], s_l.at[1], r_l.at[1], (r, sib))

    def pass_y():
        return remote(left.at[3], left.at[2 + 2 * kap], s_l.at[2], r_l.at[2], (r, sib))

    def came_y():
        part = left.at[4 - 2 * kap]
        return remote(part, part, s_l.at[2], r_l.at[2], (r, sib))

    def send_meta(steps):
        return remote(meta, ml.at[steps], s_ml.at[steps - 1], r_ml.at[steps - 1], (r, back(steps)))


    def arrived0(piece, half):
        along_x(0, piece, half, 0).start()
        along_x(0, piece, half, 1).start()

        @pl.when(jnp.logical_and(top, piece >= 4))
        def _():
            for copy in inject(piece, half, 0):
                copy.start()

        @pl.when(jnp.logical_and(bottom, piece < 4))
        def _():
            for copy in inject(piece, half, 1):
                copy.start()

    def z_step(k):
        for way in (0, 1):
            piece = z - k if way == 0 else z + k

            @pl.when(piece >= 0 if way == 0 else piece < NZ)
            def _():
                for half in (0, 1):
                    copies = along_z(piece, half, way)
                    for copy in copies:
                        copy.wait_recv()

                    @pl.when(up if way == 0 else down)
                    def _():
                        for copy in copies:
                            copy.start()

                    arrived0(piece, half)

    def chain_order(k, way):
        return k - 1 - BEHIND - (deep if way == 0 else 3 - deep)

    def chain_on(way):
        return deep < 3 if way == 0 else deep > 0

    def chain_step(k):
        for way in (0, 1):
            order = chain_order(k, way)
            piece = 7 - order if way == 0 else order

            @pl.when(jnp.logical_and(order >= 0, order < 4))
            def _():
                for half in (0, 1):
                    copies = chain(piece, half, way)
                    for copy in copies:
                        copy.wait_recv()

                    @pl.when(chain_on(way))
                    def _():
                        for copy in copies:
                            copy.start()

                    along_x(1, piece, half, 0).start()
                    along_x(1, piece, half, 1).start()

    def x_piece(tile, piece):
        for way in (0, 1):
            came_x(tile, piece, way, way).wait_recv()
            onward(tile, piece, way).start()

    def x_step(k):
        @pl.when(k == 0)
        def _():
            x_piece(0, z)

        for way in (0, 1):
            piece = z - k if way == 0 else z + k

            @pl.when(jnp.logical_and(k > 0, piece >= 0 if way == 0 else piece < NZ))
            def _():
                x_piece(0, piece)

        for way in (0, 1):
            order = chain_order(k, way)

            @pl.when(jnp.logical_and(order >= 0, order < 4))
            def _():
                x_piece(1, 7 - order if way == 0 else order)

    @pl.when(source)
    def _():
        for copy in keep():
            copy.start()
        for step in (1, 2, 3):
            for copy in scatter(step):
                copy.start()

    for steps in range(1, 6):
        send_meta(steps).start()
    for u in range(4):
        if CROSS_AT[u] == 0:
            cross(u).start()
    send_y().start()

    @pl.when(kap == 1)
    def _():
        send_own().start()

    own_meta = pltpu.make_async_copy(meta, ml.at[0], local.at[2])
    own_meta.start()

    @pl.when(source)
    def _():
        for copy in keep():
            copy.wait()

    @pl.when(jnp.logical_not(source))
    def _():
        part = quarter(rv0, z, x)
        remote(part, part, s_sc.at[0], r_sc.at[0], (r, sib)).wait_recv()
        remote(m0.at[z], m0.at[z], s_scm.at[0], r_sc.at[1], (r, sib)).wait_recv()

    for half in (0, 1):

        @pl.when(up)
        def _():
            for copy in along_z(z, half, 0):
                copy.start()

        @pl.when(down)
        def _():
            for copy in along_z(z, half, 1):
                copy.start()

        arrived0(z, half)

    @pl.loop(1, STEPS + 1)
    def _(k):
        z_step(k)
        chain_step(k)
        x_step(k - LAG)
        for u in range(4):
            if CROSS_AT[u] > 0:

                @pl.when(k == CROSS_AT[u])
                def _():
                    cross(u).start()

        @pl.when(k == 6)
        def _():
            send_y().wait_recv()
            pass_y().start()

    own_meta.wait()
    for steps in range(1, 6):
        send_meta(steps).wait_recv()
    tables = [
        pltpu.make_async_copy(ml, tl, local.at[3]),
        pltpu.make_async_copy(m0, t0, local.at[4]),
        pltpu.make_async_copy(m1, t1, local.at[5]),
    ]
    for copy in tables:
        copy.start()

    @pl.loop(0, NZ)
    def _(piece):
        for way in (0, 1):
            came_x(0, piece, way, 1 - way).wait_recv()
            came_onward(0, piece, way).wait_recv()

    for copy in tables:
        copy.wait()

    @pl.when(kap == 0)
    def _():
        send_own().wait_recv()

    came_y().wait_recv()


    def picks(tile, section, inner, kept):
        group = (2 * c + 4 * tile + 2 * section + (inner >> 3)) % NZ
        table = t1 if tile else t0
        row = 2 * (inner & 7)
        first, second = table[group, 0, inner & 7], table[group, 1, inner & 7]
        base = group * 16 + row
        return [
            jnp.where(first == wanted, base, jnp.where(second == wanted, base + 1, ZERO)) for wanted in kept
        ]

    def kept_of(section, a):
        return [tl[section, 2 + t, a] for t in range(4)]

    def terms(total, lefts, rv, spots):
        lhs = jnp.concatenate(lefts, axis=1)
        parts = []
        for pair in (0, 2):
            rhs = jnp.concatenate(
                [jnp.concatenate([rv[spot[pair]], rv[spot[pair + 1]]], axis=1) for spot in spots], axis=0
            )
            parts.append(jnp.dot(lhs, rhs, preferred_element_type=jnp.float32))
        return parts if total is None else [old + new for old, new in zip(total, parts)]

    def send_square(tile, a):
        slot = jnp.where(kap == 0, 3 - 2 * tile, 1 + 2 * tile)
        to = sib if tile == 1 else jnp.where(kap == 0, back(3), sib)
        rows = pl.ds(4 * a, 4)
        return remote(sv.at[2 * tile, rows], sv.at[slot, rows], s_sq.at[tile, a], r_sq.at[slot, a], (r, to))

    def came_square(slot, a):
        rows = pl.ds(4 * a, 4)
        return remote(sv.at[slot, rows], sv.at[slot, rows], s_sq.at[0, a], r_sq.at[slot, a], (r, sib))

    def square(tile, a):
        kept = kept_of(2 * tile, a)
        total = None
        for section in range(4):
            place = 2 * tile + section
            spots = [picks(tile, section, tl[place, i, a], kept) for i in range(2)]
            lefts = [d[2 * a + i] if place == 0 else left[place - 1, 2 * a + i] for i in range(2)]
            total = terms(total, lefts, rv1 if tile else rv0, spots)
        for t in range(4):
            sv[2 * tile, 4 * a + t] = total[t // 2][:, (t % 2) * BS : (t % 2 + 1) * BS].astype(jnp.bfloat16)
        send_square(tile, a).start()

    def cube(sections, a, total):
        kept = kept_of(0, a)
        for section in sections:
            inner = kept_of(section, a)
            for i in (0, 2):
                spots = [picks(0, section, inner[i + e], kept) for e in range(2)]
                total = terms(total, [sv[section, 4 * a + i + e] for e in range(2)], rv0, spots)
        return total

    def keep_total(a, total):
        acc[a, 0] = total[0]
        acc[a, 1] = total[1]

    @pl.loop(0, 4)
    def _(u):
        cross(u).wait_recv()
        pass_cross(u).start()

        @pl.when(kap == 0)
        def _():
            pass_cross_y(u).start()

        came_pass(u).wait_recv()
        for a in (2 * u, 2 * u + 1):
            square(0, a)
        for a in (2 * u, 2 * u + 1):
            keep_total(a, cube((0,), a, None))

    @pl.loop(0, NZ)
    def _(piece):
        for way in (0, 1):
            came_x(1, piece, way, 1 - way).wait_recv()
            came_onward(1, piece, way).wait_recv()

    @pl.loop(0, 4)
    def _(u):
        @pl.when(kap == 1)
        def _():
            pass_cross_y(u).wait_recv()

        for a in (2 * u, 2 * u + 1):
            square(1, a)

    @pl.loop(0, 8)
    def _(a):
        keep_total(a, cube((2,), a, [acc[a, 0], acc[a, 1]]))


    @pl.loop(0, NZ)
    def _(piece):
        for way in (0, 1):
            for tile in (0, 1):
                along_x(tile, piece, 0, way).wait_send()
                along_x(tile, piece, 1, way).wait_send()
                onward(tile, piece, way).wait_send()

            @pl.when(jnp.logical_and(up, piece <= z) if way == 0 else jnp.logical_and(down, piece >= z))
            def _():
                for half in (0, 1):
                    for copy in along_z(piece, half, way):
                        copy.wait_send()

            mine = piece >= 4 if way == 0 else piece < 4

            @pl.when(jnp.logical_and(chain_on(way), mine))
            def _():
                for half in (0, 1):
                    for copy in chain(piece, half, way):
                        copy.wait_send()

            @pl.when(jnp.logical_and(top if way == 0 else bottom, mine))
            def _():
                for half in (0, 1):
                    for copy in inject(piece, half, way):
                        copy.wait_send()

    for u in range(4):
        cross(u).wait_send()
        pass_cross(u).wait_send()
    for steps in range(1, 6):
        send_meta(steps).wait_send()

    @pl.when(source)
    def _():
        for step in (1, 2, 3):
            for copy in scatter(step):
                copy.wait_send()

    send_y().wait_send()
    pass_y().wait_send()

    @pl.when(kap == 1)
    def _():
        send_own().wait_send()

    @pl.when(kap == 0)
    def _():
        for u in range(4):
            pass_cross_y(u).wait_send()

    @pl.loop(0, 8)
    def _(a):
        came_square(1, a).wait_recv()
        came_square(3, a).wait_recv()
        total = cube((1, 3), a, [acc[a, 0], acc[a, 1]])
        for t in range(4):
            part = total[t // 2][:, (t % 2) * BS : (t % 2 + 1) * BS]
            out[4 * a + t] = (3.0 * sv[0, 4 * a + t].astype(jnp.float32) - 2.0 * part).astype(jnp.bfloat16)
        send_square(0, a).wait_send()
        send_square(1, a).wait_send()


def on_device(density, pattern, kept_pattern):
    own = density.reshape(16, BS, BS)
    dma = pltpu.SemaphoreType.DMA
    vmem = pl.BlockSpec(memory_space=pltpu.VMEM)
    blocks = lambda *shape: pltpu.VMEM(shape + (BS, BS), jnp.bfloat16)
    table = lambda space, count: space((count, 8, BS), jnp.int32)
    out = pl.pallas_call(
        kernel,
        out_shape=jax.ShapeDtypeStruct((32, BS, BS), jnp.bfloat16),
        in_specs=[vmem, vmem, pl.BlockSpec(memory_space=pltpu.HBM)],
        out_specs=vmem,
        scratch_shapes=[
            pltpu.VMEM((8, BS), jnp.int32),
            blocks(16),
            blocks(5, 16),
            blocks(ZERO + 1),
            blocks(ZERO + 1),
            blocks(4, 32),
            pltpu.VMEM((8, 2, BS, 2 * BS), jnp.float32),
            table(pltpu.VMEM, 6),
            table(pltpu.VMEM, NZ),
            table(pltpu.VMEM, NZ),
            table(pltpu.SMEM, 6),
            table(pltpu.SMEM, NZ),
            table(pltpu.SMEM, NZ),
            dma((3,)),
            dma((3,)),
            dma((2,)),
            dma((7,)),
            dma((NZ, 2, 2)),
            dma((NZ, 2)),
            dma((NZ, 2)),
            dma((NZ,)),
            dma((NZ, 2, 2)),
            dma((NZ, 2)),
            dma((NZ, 2)),
            dma((NZ, 2)),
            dma((NZ,)),
            dma((NZ,)),
            dma((NZ, 2, 2)),
            dma((NZ, 2, 2)),
            dma((NZ, 2)),
            dma((NZ, 2)),
            dma((NZ, 2, 2)),
            dma((NZ, 2, 2)),
            dma((NZ, 2)),
            dma((NZ, 2)),
            dma((4,)),
            dma((4,)),
            dma((4,)),
            dma((4,)),
            dma((4,)),
            dma((4,)),
            dma((3,)),
            dma((3,)),
            dma((5,)),
            dma((5,)),
            dma((2, 8)),
            dma((4, 8)),
        ],
        compiler_params=pltpu.CompilerParams(
            collective_id=0, has_side_effects=True, vmem_limit_bytes=40 << 20
        ),
        cost_estimate=pl.CostEstimate(flops=4 << 30, bytes_accessed=12 << 20, transcendentals=0),
        name="purify",
    )(pattern[:, 0].T, kept_pattern[:, 0].T, own)
    return out.reshape(8, 1, 4, BS, BS)


def solution(mesh):
    in_specs = (P("row", "col", None, None, None), P("row", "col", None), P("row", "col", None))
    out_specs = P("row", "col", None, None, None)
    return jax.shard_map(
        on_device, mesh=mesh, in_specs=in_specs, out_specs=out_specs, check_vma=False
    )
```
